512 devices in a mesh: dp: 32 (over z, y_hi), fsdp: 16 (over x, y_lo, core).
Axes of the slice: x: 4, y: 8 (y_hi: 4, y_lo: 2; y = y_hi * 2 + y_lo), z: 8, core: 2. Of those that a mesh axis runs over, the one named last changes fastest.
Arguments:
- tokens: bfloat16 [12288, 4096], P('dp', 'fsdp'), may hold values from -6 to 6
- gate_logits: bfloat16 [12288, 14336], P('dp', 'fsdp'), may hold values from -8 to 8
- linear_values: bfloat16 [12288, 14336], P('dp', 'fsdp'), may hold values from -6 to 6
- hidden_grad: bfloat16 [12288, 14336], P('dp', 'fsdp'), may hold values from -3 to 3
- basis: bfloat16 [4096, 512], P('fsdp'), may hold values from -0.09375 to 0.09375
- gate_moment: float32 [512, 14336], P('dp', 'fsdp'), may hold values from -0.75 to 0.75
- gate_second: float32 [512, 14336], P('dp', 'fsdp'), may hold values from 0.05 to 1
- linear_moment: float32 [512, 14336], P('dp', 'fsdp'), may hold values from -0.75 to 0.75
- linear_second: float32 [512, 14336], P('dp', 'fsdp'), may hold values from 0.05 to 1
Outputs:
- gate_update: float32 [4096, 14336], P('dp', 'fsdp')
- linear_update: float32 [4096, 14336], P('dp', 'fsdp')
- moment_gate: float32 [512, 14336], P('dp', 'fsdp')
- second_gate: float32 [512, 14336], P('dp', 'fsdp')
- moment_linear: float32 [512, 14336], P('dp', 'fsdp')
- second_linear: float32 [512, 14336], P('dp', 'fsdp')
The draws below stay inside these ranges and needn't reach their ends.
All inputs are finite; a program needn't handle non-finite values.
Results may differ from the reference program's by a relative error of at most 0.0057.
Values may be sent and summed in bfloat16 or wider, within the bound.
A program may use at most 64 MiB of HBM per device.

```python
import math
import jax
import jax.numpy as jnp
from jax import lax

D = 4096
FF = 14336
RANK = 512
TOKENS = 12288
N_FSDP = 16


def levels(own_key, dims, shards, smallest, top_value):
    level, own = 1.0, jax.random.fold_in(own_key, 6)
    for position, shards_of in shards:
        heights = jnp.exp(jax.random.uniform(jax.random.fold_in(own, position), (shards_of,), jnp.float32, smallest / len(shards), top_value / len(shards)))
        level = level * jnp.repeat(heights, dims[position] // shards_of).reshape([-1 if axis == position else 1 for axis in range(len(dims))])
    return level


def gaussian(key, extent, deviation, reach, pieces=(), kind=jnp.bfloat16):
    values = deviation * jax.random.normal(key, extent, jnp.float32)
    if pieces:
        values = values * levels(key, extent, pieces, -0.22, 0.18)
    return jnp.clip(values, -reach, reach).astype(kind)


def setup_inputs(seed: int = 0) -> dict:
    arg_keys = jax.random.split(jax.random.key(seed), 10)
    return {
        "tokens": gaussian(arg_keys[0], (TOKENS, D), 1.0, 6.0, ((0, 32), (1, 16))),
        "gate_logits": gaussian(arg_keys[1], (TOKENS, FF), 1.5, 8.0, ((0, 32), (1, 16))),
        "linear_values": gaussian(arg_keys[2], (TOKENS, FF), 1.0, 6.0, ((0, 32), (1, 16))),
        "hidden_grad": gaussian(arg_keys[3], (TOKENS, FF), (24.0 * TOKENS ** -0.5), 3.0, ((0, 32), (1, 16))),
        "basis": gaussian(arg_keys[4], (D, RANK), D ** -0.5, 0.09375, ((0, 16),)),
        "gate_moment": gaussian(arg_keys[5], (RANK, FF), 0.05, 0.75, ((0, 32), (1, 16)), jnp.float32),
        "gate_second": jnp.clip(jnp.exp(math.log(1.0) - 2.9957323 * jax.random.uniform(arg_keys[6], (RANK, FF), jnp.float32) ** levels(arg_keys[6], (RANK, FF), ((0, 32), (1, 16)), -0.2, 0.2)), 0.05, 1.0),
        "linear_moment": gaussian(arg_keys[7], (RANK, FF), 0.05, 0.75, ((0, 32), (1, 16)), jnp.float32),
        "linear_second": jnp.clip(jnp.exp(math.log(1.0) - 2.9957323 * jax.random.uniform(arg_keys[8], (RANK, FF), jnp.float32) ** levels(arg_keys[8], (RANK, FF), ((0, 32), (1, 16)), -0.2, 0.2)), 0.05, 1.0),
    }


def gradients(gate_logits, linear_values, hidden_grad):
    logits = gate_logits.astype(jnp.float32)
    values = linear_values.astype(jnp.float32)
    incoming = hidden_grad.astype(jnp.float32)
    sigmoid_gate = jax.nn.sigmoid(logits)
    activated = logits * sigmoid_gate
    gate_grad = (incoming * values * sigmoid_gate * (1.0 + logits * (1.0 - sigmoid_gate))).astype(jnp.bfloat16)
    linear_grad = (incoming * activated).astype(jnp.bfloat16)
    return jnp.concatenate([gate_grad, linear_grad], axis=1)

def adam_step(moment, second, grad):
    moment_out = 0.9 * moment + 0.1 * grad
    second_out = 0.999 * second + 0.001 * grad * grad
    normalized = (moment_out / (jnp.sqrt(second_out) + 1e-08)).astype(jnp.bfloat16)
    return (moment_out, second_out, normalized)

def reference(tokens, gate_logits, linear_values, hidden_grad, basis, gate_moment, gate_second, linear_moment, linear_second):
    projected = jnp.dot(tokens, basis, preferred_element_type=jnp.float32).astype(jnp.bfloat16)
    width = FF // N_FSDP

    def column_block(index):
        begin = (index * width).astype(jnp.int32)
        both = gradients(lax.dynamic_slice_in_dim(gate_logits, begin, width, 1), lax.dynamic_slice_in_dim(linear_values, begin, width, 1), lax.dynamic_slice_in_dim(hidden_grad, begin, width, 1))
        return jnp.dot(projected.T, both, preferred_element_type=jnp.float32)
    blocks = lax.map(column_block, jnp.arange(N_FSDP, dtype=jnp.int32))
    gate_sub = jnp.transpose(blocks[:, :, :width], (1, 0, 2)).reshape(RANK, FF)
    linear_sub = jnp.transpose(blocks[:, :, width:], (1, 0, 2)).reshape(RANK, FF)
    moment_gate, second_gate, gate_norm = adam_step(gate_moment, gate_second, gate_sub)
    moment_linear, second_linear, linear_norm = adam_step(linear_moment, linear_second, linear_sub)
    gate_update = jnp.dot(basis, gate_norm, preferred_element_type=jnp.float32)
    linear_update = jnp.dot(basis, linear_norm, preferred_element_type=jnp.float32)
    return (gate_update, linear_update, moment_gate, second_gate, moment_linear, second_linear)
```

```python
import functools

import jax
import jax.numpy as jnp
from jax import lax
from jax.experimental import pallas as pl
from jax.experimental.pallas import tpu as pltpu
from jax.sharding import PartitionSpec as P

MESH = pl.DeviceIdType.MESH
Y_PARTS = 4
BF16 = jnp.bfloat16
F32 = jnp.float32


def gradients(logits, values, incoming):
    logits = logits.astype(F32)
    values = values.astype(F32)
    incoming = incoming.astype(F32)
    sig = 1.0 / (1.0 + jnp.exp(-logits))
    gate = incoming * values * sig * (1.0 + logits * (1.0 - sig))
    return gate.astype(BF16), (incoming * (logits * sig)).astype(BF16)


def adam_step(moment, second, grad):
    moment_out = 0.9 * moment + 0.1 * grad
    second_out = 0.999 * second + 0.001 * grad * grad
    normalized = (moment_out / (jnp.sqrt(second_out) + 1e-08)).astype(BF16)
    return moment_out, second_out, normalized


def exchange(
    n_f, n_z, n_h,
    tokens, logits, values, incoming, basis, gate_m, gate_s, lin_m, lin_s,
    norm_out, rows_out, sub_out,
    tok_v, bas_v, log_v, val_v, inc_v, mom_v, sec_v,
    part32, part, a_recv, pt, grad, acc, rs_send, rs_recv, y_send, y_recv, norm, rows_v,
    load_sem, a_ss, a_rs, c_ss, c_rs, b_ss, b_rs, rs_ss, rs_rs, y_ss, y_rs, ya_ss, ya_rs, za_ss, za_rs,
):
    me = lax.axis_index("fsdp")
    dp = lax.axis_index("dp")
    z, h = dp // n_h, dp % n_h
    width = logits.shape[1]
    n_tok = tokens.shape[0]
    rank = basis.shape[1]
    blk = rank // n_f
    chunk = rank // n_z
    half = chunk // 2
    own = chunk // n_h
    n_rows = rows_v.shape[0]

    def z_dev(step):
        return {"dp": ((z + step + n_z) % n_z) * n_h + h}

    def y_dev(k):
        return {"dp": z * n_h + (h + k) % n_h}

    loads = [
        (tokens, tok_v), (basis, bas_v), (logits, log_v), (values, val_v), (incoming, inc_v),
        (gate_m, mom_v.at[0]), (lin_m, mom_v.at[1]), (gate_s, sec_v.at[0]), (lin_s, sec_v.at[1]),
    ]
    loads = [pltpu.make_async_copy(a, b, load_sem.at[i]) for i, (a, b) in enumerate(loads)]
    for c in loads:
        c.start()

    barrier = pltpu.get_barrier_semaphore()
    peers = [{"fsdp": (me + k) % n_f} for k in range(1, n_f)]
    peers += [z_dev(1), z_dev(-1)] + [y_dev(k) for k in range(1, n_h)]
    for p in peers:
        pl.semaphore_signal(barrier, inc=1, device_id=p, device_id_type=MESH)

    loads[0].wait()
    loads[1].wait()
    bt = bas_v[...].T
    part32[...] = lax.dot_general(bt, tok_v[...], (((1,), (1,)), ((), ())), preferred_element_type=F32)
    part[...] = part32[...].astype(BF16)
    pl.semaphore_wait(barrier, len(peers))

    sends = []

    def send(src, dst, ss, rs, dev):
        c = pltpu.make_async_remote_copy(
            src_ref=src, dst_ref=dst, send_sem=ss, recv_sem=rs, device_id=dev, device_id_type=MESH
        )
        c.start()
        sends.append(c)
        return c

    a_copies = []
    for k in range(1, n_f):
        p = (me + k) % n_f
        a_copies.append(
            send(part.at[pl.ds(p * blk, blk)], a_recv.at[k], a_ss.at[k], a_rs.at[k], {"fsdp": p})
        )

    holder = dp * n_rows // bas_v.shape[0]
    local = pl.ds((dp * n_rows) % bas_v.shape[0], n_rows)

    def row_copy(k):
        return pltpu.make_async_remote_copy(
            src_ref=bas_v.at[local], dst_ref=rows_v, send_sem=b_ss.at[k], recv_sem=b_rs,
            device_id={"fsdp": (me + k) % n_f}, device_id_type=MESH,
        )

    @pl.when(me == holder)
    def _():
        for k in range(1, n_f):
            row_copy(k).start()
        rows_v[...] = bas_v[local, :]

    for c in loads[2:5]:
        c.wait()
    step_rows = 32

    def grad_rows(i, _):
        r = pl.ds(pl.multiple_of(i * step_rows, step_rows), step_rows)
        g, l = gradients(log_v[r, :], val_v[r, :], inc_v[r, :])
        grad[r, :width] = g
        grad[r, width:] = l
        return 0

    lax.fori_loop(0, n_tok // step_rows, grad_rows, 0)

    mine = pl.ds(pl.multiple_of(me * blk, blk), blk)
    total = part32[mine, :]
    for k in range(1, n_f):
        a_copies[k - 1].wait_recv()
        total += a_recv[k].astype(F32)
    pt[mine, :] = total.astype(BF16)
    c_copies = [
        send(pt.at[mine], pt.at[mine], c_ss.at[k], c_rs.at[k], {"fsdp": (me + k) % n_f})
        for k in range(1, n_f)
    ]
    for k in range(1, n_f):
        peer = (me + n_f - k) % n_f
        there = pl.ds(pl.multiple_of(peer * blk, blk), blk)
        pltpu.make_async_remote_copy(
            src_ref=pt.at[there], dst_ref=pt.at[there], send_sem=c_ss.at[k], recv_sem=c_rs.at[k],
            device_id={"fsdp": peer}, device_id_type=MESH,
        ).wait_recv()

    def rows_of(t, off=0, size=chunk):
        return pl.ds(pl.multiple_of(((t + n_z) % n_z) * chunk + off, 16), size)

    def cols(c):
        return slice(c * width, (c + 1) * width)

    def product(t, c):
        r = rows_of(t)
        acc[r, cols(c)] = jnp.dot(pt[r, :], grad[:, cols(c)], preferred_element_type=F32)

    hops = n_z // 2
    streams = 2
    ring = {}
    for s in range(hops):
        for c in range(streams):
            for t in sorted({(hops - s) % n_z, (s - hops) % n_z}):
                product(z + t, c)
            for d, sign in ((0, 1), (1, -1)):
                t = z + sign * (hops - s)
                far = slice(0, half) if d == 0 else slice(half, chunk)
                if s == 0:
                    rs_send[c, d, s, far, :] = acc[rows_of(t, d * half, half), cols(c)].astype(BF16)
                    src, dst = rs_send.at[c, d, s, far], rs_recv.at[c, d, s, far]
                else:
                    value = acc[rows_of(t), cols(c)]
                    ring[c, d, s - 1].wait_recv()
                    if s == 1:
                        near = slice(half, chunk) if d == 0 else slice(0, half)
                        rs_send[c, d, s, far, :] = (
                            value[far, :] + rs_recv[c, d, 0, far, :].astype(F32)
                        ).astype(BF16)
                        rs_send[c, d, s, near, :] = value[near, :].astype(BF16)
                    else:
                        rs_send[c, d, s] = (value + rs_recv[c, d, s - 1].astype(F32)).astype(BF16)
                    src, dst = rs_send.at[c, d, s], rs_recv.at[c, d, s]
                ring[c, d, s] = send(src, dst, rs_ss.at[c, d, s], rs_rs.at[c, d, s], z_dev(sign))

    y_copies = {}
    for c in range(streams):
        product(z, c)
        value = acc[rows_of(z), cols(c)]
        for d in range(2):
            ring[c, d, hops - 1].wait_recv()
            value += rs_recv[c, d, hops - 1].astype(F32)
        acc[rows_of(z), cols(c)] = value
        y_send[c] = value.astype(BF16)
        for k in range(1, n_h):
            there = pl.ds(pl.multiple_of(((h + k) % n_h) * own, own), own)
            y_copies[c, k] = send(
                y_send.at[c, there], y_recv.at[c, k], y_ss.at[c, k], y_rs.at[c, k], y_dev(k)
            )

    for c in loads[5:]:
        c.wait()
    my_rows = pl.ds(pl.multiple_of(dp * own, own), own)
    ya = {}
    for c in range(streams):
        value = acc[my_rows, cols(c)]
        for k in range(1, n_h):
            y_copies[c, k].wait_recv()
            value += y_recv[c, k].astype(F32)
        sub_out[:, cols(c)] = value
        norm[my_rows, cols(c)] = adam_step(mom_v[c], sec_v[c], value)[2]
        for k in range(1, n_h):
            piece = norm.at[my_rows, cols(c)]
            ya[c, k] = send(piece, piece, ya_ss.at[c, k], ya_rs.at[c, k], y_dev(k))

    def incoming_copy(piece, ss, rs):
        return pltpu.make_async_remote_copy(
            src_ref=piece, dst_ref=piece, send_sem=ss, recv_sem=rs, device_id=z_dev(1), device_id_type=MESH
        )

    for s in range(hops + 1):
        for c in range(streams):
            if s == 0:
                for k in range(1, n_h):
                    r = pl.ds(pl.multiple_of(z * chunk + ((h + n_h - k) % n_h) * own, own), own)
                    incoming_copy(norm.at[r, cols(c)], ya_ss.at[c, k], ya_rs.at[c, k]).wait_recv()
            for d, sign in ((0, 1), (1, -1)):
                if s > 0:
                    r = rows_of(z - sign * s) if s < hops else rows_of(z - sign * s, d * half, half)
                    incoming_copy(norm.at[r, cols(c)], za_ss.at[c, d, s - 1], za_rs.at[c, d, s - 1]).wait_recv()
                if s < hops:
                    r = rows_of(z - sign * s) if s < hops - 1 else rows_of(z - sign * s, d * half, half)
                    piece = norm.at[r, cols(c)]
                    send(piece, piece, za_ss.at[c, d, s], za_rs.at[c, d, s], z_dev(sign))

    @pl.when(me != holder)
    def _():
        pltpu.make_async_remote_copy(
            src_ref=rows_v, dst_ref=rows_v, send_sem=b_ss.at[0], recv_sem=b_rs,
            device_id={"fsdp": holder}, device_id_type=MESH,
        ).wait_recv()

    @pl.when(me == holder)
    def _():
        for k in range(1, n_f):
            row_copy(k).wait_send()

    norm_out[...] = norm[...]
    rows_out[...] = rows_v[...]
    for c in sends:
        c.wait_send()


def per_device(n_f, n_dp, tokens, logits, values, incoming, basis, gate_m, gate_s, lin_m, lin_s):
    n_h = Y_PARTS
    n_z = n_dp // n_h
    n_tok, depth = tokens.shape
    width = logits.shape[1]
    rank = basis.shape[1]
    own = rank // n_dp
    chunk = rank // n_z
    n_rows = basis.shape[0] * n_f // n_dp
    hops = n_z // 2
    dma = pltpu.SemaphoreType.DMA
    anyspace = pl.BlockSpec(memory_space=pl.ANY)
    vmem = pl.BlockSpec(memory_space=pltpu.VMEM)
    norm, rows, sub = pl.pallas_call(
        functools.partial(exchange, n_f, n_z, n_h),
        out_shape=(
            jax.ShapeDtypeStruct((rank, 2 * width), BF16),
            jax.ShapeDtypeStruct((n_rows, rank), BF16),
            jax.ShapeDtypeStruct((own, 2 * width), F32),
        ),
        in_specs=[anyspace] * 9,
        out_specs=(vmem,) * 3,
        scratch_shapes=[
            pltpu.VMEM((n_tok, depth), BF16),
            pltpu.VMEM(basis.shape, BF16),
            pltpu.VMEM((n_tok, width), BF16),
            pltpu.VMEM((n_tok, width), BF16),
            pltpu.VMEM((n_tok, width), BF16),
            pltpu.VMEM((2, own, width), F32),
            pltpu.VMEM((2, own, width), F32),
            pltpu.VMEM((rank, n_tok), F32),
            pltpu.VMEM((rank, n_tok), BF16),
            pltpu.VMEM((n_f, rank // n_f, n_tok), BF16),
            pltpu.VMEM((rank, n_tok), BF16),
            pltpu.VMEM((n_tok, 2 * width), BF16),
            pltpu.VMEM((rank, 2 * width), F32),
            pltpu.VMEM((2, 2, hops, chunk, width), BF16),
            pltpu.VMEM((2, 2, hops, chunk, width), BF16),
            pltpu.VMEM((2, chunk, width), BF16),
            pltpu.VMEM((2, n_h, own, width), BF16),
            pltpu.VMEM((rank, 2 * width), BF16),
            pltpu.VMEM((n_rows, rank), BF16),
            dma((9,)),
            dma((n_f,)), dma((n_f,)),
            dma((n_f,)), dma((n_f,)),
            dma((n_f,)), dma,
            dma((2, 2, hops)), dma((2, 2, hops)),
            dma((2, n_h)), dma((2, n_h)),
            dma((2, n_h)), dma((2, n_h)),
            dma((2, 2, hops)), dma((2, 2, hops)),
        ],
        compiler_params=pltpu.CompilerParams(
            collective_id=0, has_side_effects=True, vmem_limit_bytes=48 * 1024 * 1024
        ),
    )(tokens, logits, values, incoming, basis, gate_m, gate_s, lin_m, lin_s)
    moment_gate, second_gate, _ = adam_step(gate_m, gate_s, sub[:, :width])
    moment_lin, second_lin, _ = adam_step(lin_m, lin_s, sub[:, width:])
    gate_update = jnp.dot(rows, norm[:, :width], preferred_element_type=F32)
    lin_update = jnp.dot(rows, norm[:, width:], preferred_element_type=F32)
    return gate_update, lin_update, moment_gate, second_gate, moment_lin, second_lin


def solution(mesh):
    both = P("dp", "fsdp")
    return jax.shard_map(
        functools.partial(per_device, mesh.shape["fsdp"], mesh.shape["dp"]),
        mesh=mesh,
        in_specs=(both, both, both, both, P("fsdp", None), both, both, both, both),
        out_specs=(both,) * 6,
        check_vma=False,
    )
```

```python
import functools

import jax
import jax.numpy as jnp
from jax import lax
from jax.experimental import pallas as pl
from jax.experimental.pallas import tpu as pltpu
from jax.sharding import PartitionSpec as P

MESH = pl.DeviceIdType.MESH
Y_PARTS = 4
BF16 = jnp.bfloat16
F32 = jnp.float32
STREAMS = ((0, 512, "z"), (512, 384, "y"), (896, 640, "z"), (1536, 256, "y"))


def gradients(logits, values, incoming):
    logits = logits.astype(F32)
    values = values.astype(F32)
    incoming = incoming.astype(F32)
    sig = 1.0 / (1.0 + jnp.exp(-logits))
    gate = incoming * values * sig * (1.0 + logits * (1.0 - sig))
    return gate.astype(BF16), (incoming * (logits * sig)).astype(BF16)


def exchange(
    n_f, n_z, n_h,
    tokens, logits, values, incoming, basis, gate_m, gate_s, lin_m, lin_s,
    gate_u, lin_u, gate_mo, gate_so, lin_mo, lin_so,
    tok_v, bas_v, bt_v, log_v, val_v, inc_v, mom_v, sec_v,
    part_sib, part_own, core_recv, chip_sum, a_recv, pt, grad, norm, rows_v, upd,
    load_sem, store_sem, ss, rs, b_ss, b_rs, *bufs,
):
    me = lax.axis_index("fsdp")
    dp = lax.axis_index("dp")
    z, h = dp // n_h, dp % n_h
    core, chip = me % 2, me // 2
    n_chip = n_f // 2
    width = logits.shape[1]
    n_tok = tokens.shape[0]
    rank = basis.shape[1]
    own = rank // (n_z * n_h)
    blk = rank // n_f
    n_rows = rows_v.shape[0]
    sibling = {"fsdp": chip * 2 + 1 - core}

    def z_dev(step):
        return {"dp": ((z + step + n_z) % n_z) * n_h + h}

    def y_dev(step):
        return {"dp": z * n_h + (h + step + n_h) % n_h}

    def chip_dev(k):
        return {"fsdp": ((chip + k) % n_chip) * 2 + core}

    gate_c, lin_c = slice(0, width), slice(width, 2 * width)
    loads = [
        (tokens, tok_v), (basis, bas_v), (logits, log_v), (values, val_v), (incoming, inc_v),
        (gate_m, mom_v.at[:, gate_c]), (lin_m, mom_v.at[:, lin_c]),
        (gate_s, sec_v.at[:, gate_c]), (lin_s, sec_v.at[:, lin_c]),
    ]
    loads = [pltpu.make_async_copy(a, b, load_sem.at[i]) for i, (a, b) in enumerate(loads)]
    for c in loads:
        c.start()

    barrier = pltpu.get_barrier_semaphore()
    peers = [sibling] + [chip_dev(k) for k in range(1, n_chip)]
    peers += [z_dev(k) for k in range(1, n_z)] + [y_dev(k) for k in range(1, n_h)]
    for p in peers:
        pl.semaphore_signal(barrier, inc=1, device_id=p, device_id_type=MESH)

    sends = []

    def send(src, dst, dev):
        i = len(sends)
        c = pltpu.make_async_remote_copy(
            src_ref=src, dst_ref=dst, send_sem=ss.at[i], recv_sem=rs.at[i], device_id=dev, device_id_type=MESH
        )
        c.start()
        sends.append(c)
        return c

    loads[1].wait()
    half_rank = rank // 2
    bt_v[...] = bas_v[...].T.reshape(2, half_rank, bas_v.shape[0])
    loads[0].wait()

    def project(which):
        p = lax.dot_general(bt_v[which], tok_v[...], (((1,), (1,)), ((), ())), preferred_element_type=F32)
        return p.reshape(n_chip, blk, n_tok)

    part_sib[...] = project(1 - core)
    pl.semaphore_wait(barrier, len(peers))
    core_copy = send(part_sib, core_recv, sibling)
    part_own[...] = project(core)
    core_copy.wait_recv()
    for q in range(n_chip):
        part_own[q] += core_recv[q]
    chip_sum[...] = part_own[...].astype(BF16)
    a_copies = [send(chip_sum.at[(chip + k) % n_chip], a_recv.at[k], chip_dev(k)) for k in range(1, n_chip)]

    for c in loads[2:5]:
        c.wait()
    step_rows = 32

    def grad_rows(i, _):
        r = pl.ds(pl.multiple_of(i * step_rows, step_rows), step_rows)
        g, l = gradients(log_v[r, :], val_v[r, :], inc_v[r, :])
        grad[r, gate_c] = g
        grad[r, lin_c] = l
        return 0

    lax.fori_loop(0, n_tok // step_rows, grad_rows, 0)

    per = n_h * own // blk
    cuts = blk // own
    block = core * n_chip + chip
    mine = pt.at[block // per, pl.ds((block % per) * cuts, cuts)]
    total = part_own[chip]
    for k in range(1, n_chip):
        a_copies[k - 1].wait_recv()
        total += a_recv[k].astype(F32)
    mine[...] = total.astype(BF16).reshape(cuts, own, n_tok)
    c_copies = [send(mine, mine, chip_dev(k)) for k in range(1, n_chip)]
    for c in c_copies:
        c.wait_recv()
    my_half = pt.at[pl.ds(core * (n_z // 2), n_z // 2)]
    send(my_half, my_half, sibling).wait_recv()

    holder = dp * n_rows // bas_v.shape[0]
    local = pl.ds(pl.multiple_of((dp * n_rows) % bas_v.shape[0], n_rows), n_rows)
    hx, hy, hc = holder // 4, (holder // 2) % 2, holder % 2
    fx, fy = me // 4, (me // 2) % 2
    same_core = core == hc
    is_0 = me == holder
    is_1 = same_core & (fy == hy) & (fx != hx)
    is_2 = same_core & (fy != hy)
    is_3 = core != hc

    def row_copy(i, dev):
        return pltpu.make_async_remote_copy(
            src_ref=rows_v, dst_ref=rows_v, send_sem=b_ss.at[i], recv_sem=b_rs, device_id=dev, device_id_type=MESH
        )

    def down(i):
        return row_copy(i, {"fsdp": (me + 4 * (i + 1)) % n_f})

    to_core = row_copy(n_f // 4, sibling)
    to_y = row_copy(n_f // 4 - 1, {"fsdp": fx * 4 + (1 - fy) * 2 + core})
    n_down = n_f // 4 - 1

    def rows_stream():
        yield 0.1

        @pl.when(is_0)
        def _():
            rows_v[...] = bas_v[local, :]
            for i in range(n_down):
                down(i).start()
            to_y.start()
            to_core.start()

        yield 6.0

        @pl.when(is_1)
        def _():
            to_y.wait_recv()
            to_y.start()
            to_core.start()

        yield 10.0

        @pl.when(is_2)
        def _():
            to_core.wait_recv()
            to_core.start()

        yield 14.0

        @pl.when(is_3)
        def _():
            to_core.wait_recv()

    def columns(first, size):
        return slice(first, first + size)

    def own_step(cs, value):
        moment = 0.9 * mom_v[:, cs] + 0.1 * value
        second = 0.999 * sec_v[:, cs] + 0.001 * value * value
        mom_v[:, cs] = moment
        sec_v[:, cs] = second
        norm[z, h, :, cs] = (moment / (jnp.sqrt(second) + 1e-08)).astype(BF16)

    stores = []

    def expand(first, size):
        cs = columns(first, size)
        upd[:, cs] = jnp.dot(
            rows_v[...], norm[:, :, :, cs].reshape(rank, size), preferred_element_type=F32
        )
        out, at = (gate_u, first) if first < width else (lin_u, first - width)
        c = pltpu.make_async_copy(upd.at[:, cs], out.at[:, at : at + size], store_sem.at[len(stores)])
        c.start()
        stores.append(c)

    def stream(first, size, axis, lag, buf):
        acc, ring_s, ring_r, dir_s, dir_r = buf
        cs = columns(first, size)
        z_first = axis == "z"
        n1, n2 = (n_z, n_h) if z_first else (n_h, n_z)
        p1, p2 = (z, h) if z_first else (h, z)
        dev1, dev2 = (z_dev, y_dev) if z_first else (y_dev, z_dev)
        hops = n1 // 2
        cut = n2 // 2
        far = (slice(0, cut), slice(cut, n2))
        times = (
            ([2, 5, 8, 11, 13, 15, 18, 21, 24, 26] if z_first else [4, 10.5, 13.5, 16.5, 23, 27])
        )
        when = iter([t + lag for t in times])

        def product(slot, t):
            lhs = (pt[t] if z_first else pt[:, t]).reshape(n2 * own, n_tok)
            acc[slot] = jnp.dot(lhs, grad[:, cs], preferred_element_type=F32).reshape(n2, own, size)

        def piece(t, part=slice(0, n2)):
            if z_first:
                return norm.at[t, part, :, cs]
            return norm.at[part, t, :, cs]

        ring = {}
        for s in range(hops):
            for d in range(1 if s == 0 else 2):
                sign = 1 - 2 * d
                product(d, (p1 + sign * (hops - s) + n1) % n1)
            if s > 0:
                yield next(when)
            for d in range(2):
                sign = 1 - 2 * d
                f = far[d]
                if s == 0:
                    ring_s[d, s, f] = acc[0, f].astype(BF16)
                    ring[d, s] = send(ring_s.at[d, s, f], ring_r.at[d, s, f], dev1(sign))
                    continue
                ring[d, s - 1].wait_recv()
                if s == 1:
                    n = far[1 - d]
                    ring_s[d, s, f] = (acc[d, f] + ring_r[d, 0, f].astype(F32)).astype(BF16)
                    ring_s[d, s, n] = acc[d, n].astype(BF16)
                else:
                    ring_s[d, s] = (acc[d] + ring_r[d, s - 1].astype(F32)).astype(BF16)
                ring[d, s] = send(ring_s.at[d, s], ring_r.at[d, s], dev1(sign))
        product(0, p1)
        yield next(when)
        for d in range(2):
            ring[d, hops - 1].wait_recv()
        acc[0] = acc[0] + ring_r[0, hops - 1].astype(F32) + ring_r[1, hops - 1].astype(F32)
        dir_s[...] = acc[0].astype(BF16)
        direct = [send(dir_s.at[(p2 + k) % n2], dir_r.at[k], dev2(k)) for k in range(1, n2)]
        yield next(when)
        value = acc[0, p2]
        for k in range(1, n2):
            direct[k - 1].wait_recv()
            value += dir_r[k].astype(F32)
        own_step(cs, value)
        mine = norm.at[z, h, :, cs]
        direct = [send(mine, mine, dev2(k)) for k in range(1, n2)]
        yield next(when)
        for c in direct:
            c.wait_recv()
        back = {}
        for s in range(hops):
            for d in range(2):
                sign = 1 - 2 * d
                if s > 0:
                    back[d, s - 1].wait_recv()
                t = (p1 - sign * s + n1) % n1
                p = piece(t) if s < hops - 1 else piece(t, far[d])
                back[d, s] = send(p, p, dev1(sign))
            yield next(when)
        for d in range(2):
            back[d, hops - 1].wait_recv()
        expand(first, size)

    for c in loads[5:]:
        c.wait()
    lanes = [stream(f, w, axis, i * 0.5, bufs[5 * i : 5 * i + 5]) for i, (f, w, axis) in enumerate(STREAMS)]
    lanes.append(rows_stream())
    queue = [(next(g), i, g) for i, g in enumerate(lanes)]
    while queue:
        queue.sort(key=lambda e: e[:2])
        _, i, g = queue.pop(0)
        t = next(g, None)
        if t is not None:
            queue.append((t, i, g))

    outs = [
        (mom_v.at[:, gate_c], gate_mo), (sec_v.at[:, gate_c], gate_so),
        (mom_v.at[:, lin_c], lin_mo), (sec_v.at[:, lin_c], lin_so),
    ]
    for a, b in outs:
        c = pltpu.make_async_copy(a, b, store_sem.at[len(stores)])
        c.start()
        stores.append(c)

    @pl.when(is_0)
    def _():
        for i in range(n_down):
            down(i).wait_send()

    @pl.when(is_0 | is_1)
    def _():
        to_y.wait_send()

    @pl.when(same_core)
    def _():
        to_core.wait_send()

    for c in sends:
        c.wait_send()
    for c in stores:
        c.wait()


def copy_out(n, *refs):
    stage, sem = refs[2 * n : 3 * n], refs[-1]
    reads = [pltpu.make_async_copy(refs[i], stage[i], sem.at[i]) for i in range(n)]
    writes = [pltpu.make_async_copy(stage[i], refs[n + i], sem.at[n + i]) for i in range(n)]
    for c in reads:
        c.start()
    for r, w in zip(reads, writes):
        r.wait()
        w.start()
    for c in writes:
        c.wait()


def per_device(n_f, n_dp, tokens, logits, values, incoming, basis, gate_m, gate_s, lin_m, lin_s):
    n_h = Y_PARTS
    n_z = n_dp // n_h
    n_tok, depth = tokens.shape
    width = logits.shape[1]
    rank = basis.shape[1]
    own = rank // n_dp
    n_rows = basis.shape[0] * n_f // n_dp
    blk = rank // n_f
    dma = pltpu.SemaphoreType.DMA
    hbm = pl.BlockSpec(memory_space=pltpu.HBM)
    bufs = []
    for _, size, axis in STREAMS:
        n1, n2 = (n_z, n_h) if axis == "z" else (n_h, n_z)
        bufs += [
            pltpu.VMEM((2, n2, own, size), F32),
            pltpu.VMEM((2, n1 // 2, n2, own, size), BF16),
            pltpu.VMEM((2, n1 // 2, n2, own, size), BF16),
            pltpu.VMEM((n2, own, size), BF16),
            pltpu.VMEM((n2, own, size), BF16),
        ]
    outs = tuple(
        jax.ShapeDtypeStruct((r, width), F32) for r in (n_rows, n_rows, own, own, own, own)
    )
    done = pl.pallas_call(
        functools.partial(exchange, n_f, n_z, n_h),
        out_shape=outs,
        in_specs=[hbm] * 9,
        out_specs=(hbm,) * 6,
        scratch_shapes=[
            pltpu.VMEM((n_tok, depth), BF16),
            pltpu.VMEM(basis.shape, BF16),
            pltpu.VMEM((2, rank // 2, depth), BF16),
            pltpu.VMEM((n_tok, width), BF16),
            pltpu.VMEM((n_tok, width), BF16),
            pltpu.VMEM((n_tok, width), BF16),
            pltpu.VMEM((own, 2 * width), F32),
            pltpu.VMEM((own, 2 * width), F32),
            pltpu.VMEM((n_f // 2, blk, n_tok), F32),
            pltpu.VMEM((n_f // 2, blk, n_tok), F32),
            pltpu.VMEM((n_f // 2, blk, n_tok), F32),
            pltpu.VMEM((n_f // 2, blk, n_tok), BF16),
            pltpu.VMEM((n_f // 2, blk, n_tok), BF16),
            pltpu.VMEM((n_z, n_h, own, n_tok), BF16),
            pltpu.VMEM((n_tok, 2 * width), BF16),
            pltpu.VMEM((n_z, n_h, own, 2 * width), BF16),
            pltpu.VMEM((n_rows, rank), BF16),
            pltpu.VMEM((n_rows, 2 * width), F32),
            dma((9,)),
            dma((len(STREAMS) + 4,)),
            dma((128,)),
            dma((128,)),
            dma((n_f // 4 + 1,)),
            dma,
            *bufs,
        ],
        compiler_params=pltpu.CompilerParams(
            collective_id=0, has_side_effects=True, vmem_limit_bytes=64 * 1024 * 1024
        ),
    )(tokens, logits, values, incoming, basis, gate_m, gate_s, lin_m, lin_s)
    gate_u, lin_u, mg, sg, ml, sl = pl.pallas_call(
        functools.partial(copy_out, 6),
        out_shape=outs,
        in_specs=[hbm] * 6,
        out_specs=(hbm,) * 6,
        scratch_shapes=[pltpu.VMEM(o.shape, F32) for o in outs] + [dma((12,))],
    )(*done)
    return gate_u, lin_u, mg, sg, ml, sl


def solution(mesh):
    both = P("dp", "fsdp")
    return jax.shard_map(
        functools.partial(per_device, mesh.shape["fsdp"], mesh.shape["dp"]),
        mesh=mesh,
        in_specs=(both, both, both, both, P("fsdp", None), both, both, both, both),
        out_specs=(both,) * 6,
        check_vma=False,
    )
```

```python
import functools

import jax
import jax.numpy as jnp
from jax import lax
from jax.experimental import pallas as pl
from jax.experimental.pallas import tpu as pltpu
from jax.sharding import PartitionSpec as P

MESH = pl.DeviceIdType.MESH
Y_PARTS = 4
BF16 = jnp.bfloat16
F32 = jnp.float32
STREAMS = ((0, 384, 'z'), (384, 384, 'y'), (768, 384, 'z'), (1152, 256, 'y'), (1408, 384, 'z'))


def gradients(logits, values, incoming):
    logits = logits.astype(F32)
    values = values.astype(F32)
    incoming = incoming.astype(F32)
    sig = 1.0 / (1.0 + jnp.exp(-logits))
    gate = incoming * values * sig * (1.0 + logits * (1.0 - sig))
    return gate.astype(BF16), (incoming * (logits * sig)).astype(BF16)


def exchange(
    n_f, n_z, n_h,
    tokens, logits, values, incoming, basis, gate_m, gate_s, lin_m, lin_s,
    gate_u, lin_u, gate_mo, gate_so, lin_mo, lin_so,
    tok_v, bas_v, bt_v, log_v, val_v, inc_v, mom_v, sec_v,
    part_sib, part_own, core_recv, chip_sum, a_recv, pt, grad, norm, rows_v, upd,
    load_sem, store_sem, ss, rs, b_ss, b_rs, *bufs,
):
    me = lax.axis_index("fsdp")
    dp = lax.axis_index("dp")
    z, h = dp // n_h, dp % n_h
    core, chip = me % 2, me // 2
    n_chip = n_f // 2
    width = logits.shape[1]
    n_tok = tokens.shape[0]
    rank = basis.shape[1]
    own = rank // (n_z * n_h)
    blk = rank // n_f
    n_rows = rows_v.shape[0]
    sibling = {"fsdp": chip * 2 + 1 - core}

    def z_dev(step):
        return {"dp": ((z + step + n_z) % n_z) * n_h + h}

    def y_dev(step):
        return {"dp": z * n_h + (h + step + n_h) % n_h}

    def chip_dev(k):
        return {"fsdp": ((chip + k) % n_chip) * 2 + core}

    gate_c, lin_c = slice(0, width), slice(width, 2 * width)
    loads = [
        (tokens, tok_v), (basis, bas_v), (logits, log_v), (values, val_v), (incoming, inc_v),
        (gate_m, mom_v.at[:, gate_c]), (lin_m, mom_v.at[:, lin_c]),
        (gate_s, sec_v.at[:, gate_c]), (lin_s, sec_v.at[:, lin_c]),
    ]
    loads = [pltpu.make_async_copy(a, b, load_sem.at[i]) for i, (a, b) in enumerate(loads)]
    for c in loads:
        c.start()

    barrier = pltpu.get_barrier_semaphore()
    peers = [sibling] + [chip_dev(k) for k in range(1, n_chip)]
    peers += [z_dev(k) for k in range(1, n_z)] + [y_dev(k) for k in range(1, n_h)]
    for p in peers:
        pl.semaphore_signal(barrier, inc=1, device_id=p, device_id_type=MESH)

    sends = []

    def send(src, dst, dev):
        i = len(sends)
        c = pltpu.make_async_remote_copy(
            src_ref=src, dst_ref=dst, send_sem=ss.at[i], recv_sem=rs.at[i], device_id=dev, device_id_type=MESH
        )
        c.start()
        sends.append(c)
        return c

    loads[1].wait()
    half_rank = rank // 2
    bt_v[...] = bas_v[...].T.reshape(2, half_rank, bas_v.shape[0])
    loads[0].wait()

    def project(which):
        p = lax.dot_general(bt_v[which], tok_v[...], (((1,), (1,)), ((), ())), preferred_element_type=F32)
        return p.reshape(n_chip, blk, n_tok)

    part_sib[...] = project(1 - core)
    pl.semaphore_wait(barrier, len(peers))
    core_copy = send(part_sib, core_recv, sibling)
    part_own[...] = project(core)
    core_copy.wait_recv()
    for q in range(n_chip):
        part_own[q] += core_recv[q]
    chip_sum[...] = part_own[...].astype(BF16)
    a_copies = [send(chip_sum.at[(chip + k) % n_chip], a_recv.at[k], chip_dev(k)) for k in range(1, n_chip)]

    for c in loads[2:5]:
        c.wait()
    step_rows = 32

    def grad_rows(i, _):
        r = pl.ds(pl.multiple_of(i * step_rows, step_rows), step_rows)
        g, l = gradients(log_v[r, :], val_v[r, :], inc_v[r, :])
        grad[r, gate_c] = g
        grad[r, lin_c] = l
        return 0

    lax.fori_loop(0, n_tok // step_rows, grad_rows, 0)

    per = n_h * own // blk
    cuts = blk // own
    block = core * n_chip + chip
    mine = pt.at[block // per, pl.ds((block % per) * cuts, cuts)]
    total = part_own[chip]
    for k in range(1, n_chip):
        a_copies[k - 1].wait_recv()
        total += a_recv[k].astype(F32)
    mine[...] = total.astype(BF16).reshape(cuts, own, n_tok)
    c_copies = [send(mine, mine, chip_dev(k)) for k in range(1, n_chip)]
    for c in c_copies:
        c.wait_recv()
    my_half = pt.at[pl.ds(core * (n_z // 2), n_z // 2)]
    send(my_half, my_half, sibling).wait_recv()

    holder = dp * n_rows // bas_v.shape[0]
    local = pl.ds(pl.multiple_of((dp * n_rows) % bas_v.shape[0], n_rows), n_rows)
    hx, hy, hc = holder // 4, (holder // 2) % 2, holder % 2
    fx, fy = me // 4, (me // 2) % 2
    same_core = core == hc
    is_0 = me == holder
    is_1 = same_core & (fy == hy) & (fx != hx)
    is_2 = same_core & (fy != hy)
    is_3 = core != hc

    def row_copy(i, dev):
        return pltpu.make_async_remote_copy(
            src_ref=rows_v, dst_ref=rows_v, send_sem=b_ss.at[i], recv_sem=b_rs, device_id=dev, device_id_type=MESH
        )

    def down(i):
        return row_copy(i, {"fsdp": (me + 4 * (i + 1)) % n_f})

    to_core = row_copy(n_f // 4, sibling)
    to_y = row_copy(n_f // 4 - 1, {"fsdp": fx * 4 + (1 - fy) * 2 + core})
    n_down = n_f // 4 - 1

    def rows_stream():
        yield 0.1

        @pl.when(is_0)
        def _():
            rows_v[...] = bas_v[local, :]
            for i in range(n_down):
                down(i).start()
            to_y.start()
            to_core.start()

        yield 6.0

        @pl.when(is_1)
        def _():
            to_y.wait_recv()
            to_y.start()
            to_core.start()

        yield 10.0

        @pl.when(is_2)
        def _():
            to_core.wait_recv()
            to_core.start()

        yield 14.0

        @pl.when(is_3)
        def _():
            to_core.wait_recv()

    def columns(first, size):
        return slice(first, first + size)

    stores, stepped = [], []

    def store(src, dst):
        c = pltpu.make_async_copy(src, dst, store_sem.at[len(stores)])
        c.start()
        stores.append(c)

    def own_step(cs, value):
        moment = 0.9 * mom_v[:, cs] + 0.1 * value
        second = 0.999 * sec_v[:, cs] + 0.001 * value * value
        mom_v[:, cs] = moment
        sec_v[:, cs] = second
        norm[z, h, :, cs] = (moment / (jnp.sqrt(second) + 1e-08)).astype(BF16)
        stepped.append(cs)
        if len(stepped) == len(STREAMS):
            store(mom_v.at[:, gate_c], gate_mo)
            store(sec_v.at[:, gate_c], gate_so)
            store(mom_v.at[:, lin_c], lin_mo)
            store(sec_v.at[:, lin_c], lin_so)

    def expand(first, size):
        cs = columns(first, size)
        upd[:, cs] = jnp.dot(
            rows_v[...], norm[:, :, :, cs].reshape(rank, size), preferred_element_type=F32
        )
        for out, low in ((gate_u, 0), (lin_u, width)):
            begin, end = max(first, low), min(first + size, low + width)
            if begin < end:
                store(upd.at[:, begin:end], out.at[:, begin - low : end - low])

    def stream(first, size, axis, lag, buf):
        acc, ring_s, ring_r, dir_s, dir_r = buf
        cs = columns(first, size)
        z_first = axis == "z"
        n1, n2 = (n_z, n_h) if z_first else (n_h, n_z)
        p1, p2 = (z, h) if z_first else (h, z)
        dev1, dev2 = (z_dev, y_dev) if z_first else (y_dev, z_dev)
        hops = n1 // 2
        cut = n2 // 2
        far = (slice(0, cut), slice(cut, n2))
        times = (
            ([2, 5, 8, 11, 13, 15, 18, 21, 24, 26] if z_first else [3, 9.5, 12.5, 15.5, 22, 26])
        )
        when = iter([t + lag for t in times])

        def product(slot, t):
            lhs = (pt[t] if z_first else pt[:, t]).reshape(n2 * own, n_tok)
            acc[slot] = jnp.dot(lhs, grad[:, cs], preferred_element_type=F32).reshape(n2, own, size)

        def piece(t, part=slice(0, n2)):
            if z_first:
                return norm.at[t, part, :, cs]
            return norm.at[part, t, :, cs]

        ring = {}
        for s in range(hops):
            for d in range(1 if s == 0 else 2):
                sign = 1 - 2 * d
                product(d, (p1 + sign * (hops - s) + n1) % n1)
            if s > 0:
                yield next(when)
            for d in range(2):
                sign = 1 - 2 * d
                f = far[d]
                if s == 0:
                    ring_s[d, s, f] = acc[0, f].astype(BF16)
                    ring[d, s] = send(ring_s.at[d, s, f], ring_r.at[d, s, f], dev1(sign))
                    continue
                ring[d, s - 1].wait_recv()
                if s == 1:
                    n = far[1 - d]
                    ring_s[d, s, f] = (acc[d, f] + ring_r[d, 0, f].astype(F32)).astype(BF16)
                    ring_s[d, s, n] = acc[d, n].astype(BF16)
                else:
                    ring_s[d, s] = (acc[d] + ring_r[d, s - 1].astype(F32)).astype(BF16)
                ring[d, s] = send(ring_s.at[d, s], ring_r.at[d, s], dev1(sign))
        product(0, p1)
        yield next(when)
        for d in range(2):
            ring[d, hops - 1].wait_recv()
        acc[0] = acc[0] + ring_r[0, hops - 1].astype(F32) + ring_r[1, hops - 1].astype(F32)
        dir_s[...] = acc[0].astype(BF16)
        direct = [send(dir_s.at[(p2 + k) % n2], dir_r.at[k], dev2(k)) for k in range(1, n2)]
        yield next(when)
        value = acc[0, p2]
        for k in range(1, n2):
            direct[k - 1].wait_recv()
            value += dir_r[k].astype(F32)
        own_step(cs, value)
        mine = norm.at[z, h, :, cs]
        direct = [send(mine, mine, dev2(k)) for k in range(1, n2)]
        yield next(when)
        for c in direct:
            c.wait_recv()
        back = {}
        for s in range(hops):
            for d in range(2):
                sign = 1 - 2 * d
                if s > 0:
                    back[d, s - 1].wait_recv()
                t = (p1 - sign * s + n1) % n1
                p = piece(t) if s < hops - 1 else piece(t, far[d])
                back[d, s] = send(p, p, dev1(sign))
            yield next(when)
        for d in range(2):
            back[d, hops - 1].wait_recv()
        expand(first, size)

    for c in loads[5:]:
        c.wait()
    lanes = [stream(f, w, axis, i * 0.3, bufs[5 * i : 5 * i + 5]) for i, (f, w, axis) in enumerate(STREAMS)]
    lanes.append(rows_stream())
    marks, settled = [], [0]

    def settle():
        marks.append(len(sends))
        if len(marks) > 2 * len(lanes):
            upto = marks[-2 * len(lanes) - 1]
            for c in sends[settled[0] : upto]:
                c.wait_send()
            settled[0] = upto

    queue = [(next(g), i, g) for i, g in enumerate(lanes)]
    while queue:
        queue.sort(key=lambda e: e[:2])
        _, i, g = queue.pop(0)
        t = next(g, None)
        if t is not None:
            queue.append((t, i, g))
        settle()

    @pl.when(is_0)
    def _():
        for i in range(n_down):
            down(i).wait_send()

    @pl.when(is_0 | is_1)
    def _():
        to_y.wait_send()

    @pl.when(same_core)
    def _():
        to_core.wait_send()

    for c in sends[settled[0] :]:
        c.wait_send()
    for c in stores:
        c.wait()


def copy_out(n, *refs):
    stage, sem = refs[2 * n : 3 * n], refs[-1]
    reads = [pltpu.make_async_copy(refs[i], stage[i], sem.at[i]) for i in range(n)]
    writes = [pltpu.make_async_copy(stage[i], refs[n + i], sem.at[n + i]) for i in range(n)]
    for c in reads:
        c.start()
    for r, w in zip(reads, writes):
        r.wait()
        w.start()
    for c in writes:
        c.wait()


def per_device(n_f, n_dp, tokens, logits, values, incoming, basis, gate_m, gate_s, lin_m, lin_s):
    n_h = Y_PARTS
    n_z = n_dp // n_h
    n_tok, depth = tokens.shape
    width = logits.shape[1]
    rank = basis.shape[1]
    own = rank // n_dp
    n_rows = basis.shape[0] * n_f // n_dp
    blk = rank // n_f
    dma = pltpu.SemaphoreType.DMA
    hbm = pl.BlockSpec(memory_space=pltpu.HBM)
    bufs = []
    n_sends = n_f
    for _, size, axis in STREAMS:
        n1, n2 = (n_z, n_h) if axis == "z" else (n_h, n_z)
        n_sends += 2 * n1 + 2 * (n2 - 1)
        bufs += [
            pltpu.VMEM((2, n2, own, size), F32),
            pltpu.VMEM((2, n1 // 2, n2, own, size), BF16),
            pltpu.VMEM((2, n1 // 2, n2, own, size), BF16),
            pltpu.VMEM((n2, own, size), BF16),
            pltpu.VMEM((n2, own, size), BF16),
        ]
    outs = tuple(
        jax.ShapeDtypeStruct((r, width), F32) for r in (n_rows, n_rows, own, own, own, own)
    )
    done = pl.pallas_call(
        functools.partial(exchange, n_f, n_z, n_h),
        out_shape=outs,
        in_specs=[hbm] * 9,
        out_specs=(hbm,) * 6,
        scratch_shapes=[
            pltpu.VMEM((n_tok, depth), BF16),
            pltpu.VMEM(basis.shape, BF16),
            pltpu.VMEM((2, rank // 2, depth), BF16),
            pltpu.VMEM((n_tok, width), BF16),
            pltpu.VMEM((n_tok, width), BF16),
            pltpu.VMEM((n_tok, width), BF16),
            pltpu.VMEM((own, 2 * width), F32),
            pltpu.VMEM((own, 2 * width), F32),
            pltpu.VMEM((n_f // 2, blk, n_tok), F32),
            pltpu.VMEM((n_f // 2, blk, n_tok), F32),
            pltpu.VMEM((n_f // 2, blk, n_tok), F32),
            pltpu.VMEM((n_f // 2, blk, n_tok), BF16),
            pltpu.VMEM((n_f // 2, blk, n_tok), BF16),
            pltpu.VMEM((n_z, n_h, own, n_tok), BF16),
            pltpu.VMEM((n_tok, 2 * width), BF16),
            pltpu.VMEM((n_z, n_h, own, 2 * width), BF16),
            pltpu.VMEM((n_rows, rank), BF16),
            pltpu.VMEM((n_rows, 2 * width), F32),
            dma((9,)),
            dma((len(STREAMS) + 5,)),
            dma((n_sends,)),
            dma((n_sends,)),
            dma((n_f // 4 + 1,)),
            dma,
            *bufs,
        ],
        compiler_params=pltpu.CompilerParams(
            collective_id=0, has_side_effects=True, vmem_limit_bytes=64 * 1024 * 1024
        ),
    )(tokens, logits, values, incoming, basis, gate_m, gate_s, lin_m, lin_s)
    gate_u, lin_u, mg, sg, ml, sl = pl.pallas_call(
        functools.partial(copy_out, 6),
        out_shape=outs,
        in_specs=[hbm] * 6,
        out_specs=(hbm,) * 6,
        scratch_shapes=[pltpu.VMEM(o.shape, F32) for o in outs] + [dma((12,))],
    )(*done)
    return gate_u, lin_u, mg, sg, ml, sl


def solution(mesh):
    both = P("dp", "fsdp")
    return jax.shard_map(
        functools.partial(per_device, mesh.shape["fsdp"], mesh.shape["dp"]),
        mesh=mesh,
        in_specs=(both, both, both, both, P("fsdp", None), both, both, both, both),
        out_specs=(both,) * 6,
        check_vma=False,
    )
```

```python
import functools

import jax
import jax.numpy as jnp
from jax import lax
from jax.experimental import pallas as pl
from jax.experimental.pallas import tpu as pltpu
from jax.sharding import PartitionSpec as P

MESH = pl.DeviceIdType.MESH
Y_PARTS = 4
BF16 = jnp.bfloat16
F32 = jnp.float32
STREAMS = ((0, 384, 'z'), (384, 384, 'y'), (768, 384, 'z'), (1152, 256, 'y'), (1408, 384, 'z'))


def gradients(logits, values, incoming):
    logits = logits.astype(F32)
    values = values.astype(F32)
    incoming = incoming.astype(F32)
    sig = 1.0 / (1.0 + jnp.exp(-logits))
    gate = incoming * values * sig * (1.0 + logits * (1.0 - sig))
    return gate.astype(BF16), (incoming * (logits * sig)).astype(BF16)


def exchange(
    n_f, n_z, n_h,
    tokens, logits, values, incoming, basis, gate_m, gate_s, lin_m, lin_s,
    gate_u, lin_u, gate_mo, gate_so, lin_mo, lin_so,
    tok_v, bas_v, bt_v, log_v, val_v, inc_v, mom_v, sec_v,
    part_sib, part_own, core_recv, chip_sum, a_recv, pt, grad, norm, rows_v, upd,
    load_sem, store_sem, ss, rs, b_ss, b_rs, *bufs,
):
    me = lax.axis_index("fsdp")
    dp = lax.axis_index("dp")
    z, h = dp // n_h, dp % n_h
    core, chip = me % 2, me // 2
    n_chip = n_f // 2
    width = logits.shape[1]
    n_tok = tokens.shape[0]
    rank = basis.shape[1]
    own = rank // (n_z * n_h)
    blk = rank // n_f
    n_rows = rows_v.shape[0]
    sibling = {"fsdp": chip * 2 + 1 - core}

    def z_dev(step):
        return {"dp": ((z + step + n_z) % n_z) * n_h + h}

    def y_dev(step):
        return {"dp": z * n_h + (h + step + n_h) % n_h}

    def chip_dev(k):
        return {"fsdp": ((chip + k) % n_chip) * 2 + core}

    gate_c, lin_c = slice(0, width), slice(width, 2 * width)
    loads = [
        (tokens, tok_v), (basis, bas_v), (logits, log_v), (values, val_v), (incoming, inc_v),
        (gate_m, mom_v.at[:, gate_c]), (lin_m, mom_v.at[:, lin_c]),
        (gate_s, sec_v.at[:, gate_c]), (lin_s, sec_v.at[:, lin_c]),
    ]
    loads = [pltpu.make_async_copy(a, b, load_sem.at[i]) for i, (a, b) in enumerate(loads)]
    for c in loads:
        c.start()

    barrier = pltpu.get_barrier_semaphore()
    peers = [sibling] + [chip_dev(k) for k in range(1, n_chip)]
    peers += [z_dev(k) for k in range(1, n_z)] + [y_dev(k) for k in range(1, n_h)]
    for p in peers:
        pl.semaphore_signal(barrier, inc=1, device_id=p, device_id_type=MESH)

    sends = []

    used = [0]

    def send(src, dst, dev):
        i = used[0]
        used[0] += 1
        c = pltpu.make_async_remote_copy(
            src_ref=src, dst_ref=dst, send_sem=ss.at[i], recv_sem=rs.at[i], device_id=dev, device_id_type=MESH
        )
        c.start()
        sends.append(c)
        return c

    def send_all(pairs, landing):
        i = used[0]
        used[0] += 1
        for src, dst, dev in pairs:
            pltpu.make_async_remote_copy(
                src_ref=src, dst_ref=dst, send_sem=ss.at[i], recv_sem=rs.at[i], device_id=dev, device_id_type=MESH
            ).start()
        whole = pltpu.make_async_remote_copy(
            src_ref=landing, dst_ref=landing, send_sem=ss.at[i], recv_sem=rs.at[i],
            device_id=sibling, device_id_type=MESH,
        )
        sends.append(whole)
        return whole

    loads[1].wait()
    half_rank = rank // 2
    bt_v[...] = bas_v[...].T.reshape(2, half_rank, bas_v.shape[0])
    loads[0].wait()

    def project(which):
        p = lax.dot_general(bt_v[which], tok_v[...], (((1,), (1,)), ((), ())), preferred_element_type=F32)
        return p.reshape(n_chip, blk, n_tok)

    part_sib[...] = project(1 - core)
    pl.semaphore_wait(barrier, len(peers))
    core_copy = send(part_sib, core_recv, sibling)
    part_own[...] = project(core)
    core_copy.wait_recv()
    for q in range(n_chip):
        part_own[q] += core_recv[q]
    chip_sum[...] = part_own[...].astype(BF16)
    others = range(1, n_chip)
    a_copy = send_all(
        [(chip_sum.at[(chip + k) % n_chip], a_recv.at[k], chip_dev(k)) for k in others], a_recv.at[1:]
    )

    for c in loads[2:5]:
        c.wait()
    step_rows = 32

    def grad_rows(i, _):
        r = pl.ds(pl.multiple_of(i * step_rows, step_rows), step_rows)
        g, l = gradients(log_v[r, :], val_v[r, :], inc_v[r, :])
        grad[r, gate_c] = g
        grad[r, lin_c] = l
        return 0

    lax.fori_loop(0, n_tok // step_rows, grad_rows, 0)

    per = n_h * own // blk
    cuts = blk // own
    block = core * n_chip + chip
    mine = pt.at[block // per, pl.ds((block % per) * cuts, cuts)]
    total = part_own[chip]
    a_copy.wait_recv()
    for k in others:
        total += a_recv[k].astype(F32)
    mine[...] = total.astype(BF16).reshape(cuts, own, n_tok)
    send_all([(mine, mine, chip_dev(k)) for k in others], a_recv.at[1:]).wait_recv()
    my_half = pt.at[pl.ds(core * (n_z // 2), n_z // 2)]
    send(my_half, my_half, sibling).wait_recv()

    holder = dp * n_rows // bas_v.shape[0]
    local = pl.ds(pl.multiple_of((dp * n_rows) % bas_v.shape[0], n_rows), n_rows)
    hx, hy, hc = holder // 4, (holder // 2) % 2, holder % 2
    fx, fy = me // 4, (me // 2) % 2
    same_core = core == hc
    is_0 = me == holder
    is_1 = same_core & (fy == hy) & (fx != hx)
    is_2 = same_core & (fy != hy)
    is_3 = core != hc

    def row_copy(i, dev):
        return pltpu.make_async_remote_copy(
            src_ref=rows_v, dst_ref=rows_v, send_sem=b_ss.at[i], recv_sem=b_rs, device_id=dev, device_id_type=MESH
        )

    def down(i):
        return row_copy(i, {"fsdp": (me + 4 * (i + 1)) % n_f})

    to_core = row_copy(n_f // 4, sibling)
    to_y = row_copy(n_f // 4 - 1, {"fsdp": fx * 4 + (1 - fy) * 2 + core})
    n_down = n_f // 4 - 1

    def rows_stream():
        yield 0.1

        @pl.when(is_0)
        def _():
            rows_v[...] = bas_v[local, :]
            for i in range(n_down):
                down(i).start()
            to_y.start()
            to_core.start()

        yield 6.0

        @pl.when(is_1)
        def _():
            to_y.wait_recv()
            to_y.start()
            to_core.start()

        yield 10.0

        @pl.when(is_2)
        def _():
            to_core.wait_recv()
            to_core.start()

        yield 14.0

        @pl.when(is_3)
        def _():
            to_core.wait_recv()

    def columns(first, size):
        return slice(first, first + size)

    stores, stepped = [], []

    def store(src, dst):
        c = pltpu.make_async_copy(src, dst, store_sem.at[len(stores)])
        c.start()
        stores.append(c)

    def own_step(cs, value):
        moment = 0.9 * mom_v[:, cs] + 0.1 * value
        second = 0.999 * sec_v[:, cs] + 0.001 * value * value
        mom_v[:, cs] = moment
        sec_v[:, cs] = second
        norm[z, h, :, cs] = (moment / (jnp.sqrt(second) + 1e-08)).astype(BF16)
        stepped.append(cs)
        if len(stepped) == len(STREAMS):
            store(mom_v.at[:, gate_c], gate_mo)
            store(sec_v.at[:, gate_c], gate_so)
            store(mom_v.at[:, lin_c], lin_mo)
            store(sec_v.at[:, lin_c], lin_so)

    def expand(first, size):
        cs = columns(first, size)
        upd[:, cs] = jnp.dot(
            rows_v[...], norm[:, :, :, cs].reshape(rank, size), preferred_element_type=F32
        )
        for out, low in ((gate_u, 0), (lin_u, width)):
            begin, end = max(first, low), min(first + size, low + width)
            if begin < end:
                store(upd.at[:, begin:end], out.at[:, begin - low : end - low])

    def stream(first, size, axis, lag, buf):
        acc, ring_s, ring_r, dir_s, dir_r = buf
        cs = columns(first, size)
        z_first = axis == "z"
        n1, n2 = (n_z, n_h) if z_first else (n_h, n_z)
        p1, p2 = (z, h) if z_first else (h, z)
        dev1, dev2 = (z_dev, y_dev) if z_first else (y_dev, z_dev)
        hops = n1 // 2
        cut = n2 // 2
        far = (slice(0, cut), slice(cut, n2))
        times = (
            ([2, 5, 8, 11, 13, 15, 18, 21, 24, 26] if z_first else [3, 9.5, 12.5, 15.5, 22, 26])
        )
        when = iter([t + lag for t in times])

        def product(slot, t):
            lhs = (pt[t] if z_first else pt[:, t]).reshape(n2 * own, n_tok)
            acc[slot] = jnp.dot(lhs, grad[:, cs], preferred_element_type=F32).reshape(n2, own, size)

        def piece(t, part=slice(0, n2)):
            if z_first:
                return norm.at[t, part, :, cs]
            return norm.at[part, t, :, cs]

        ring = {}
        for s in range(hops):
            for d in range(1 if s == 0 else 2):
                sign = 1 - 2 * d
                product(d, (p1 + sign * (hops - s) + n1) % n1)
            if s > 0:
                yield next(when)
            for d in range(2):
                sign = 1 - 2 * d
                f = far[d]
                if s == 0:
                    ring_s[d, s, f] = acc[0, f].astype(BF16)
                    ring[d, s] = send(ring_s.at[d, s, f], ring_r.at[d, s, f], dev1(sign))
                    continue
                ring[d, s - 1].wait_recv()
                if s == 1:
                    n = far[1 - d]
                    ring_s[d, s, f] = (acc[d, f] + ring_r[d, 0, f].astype(F32)).astype(BF16)
                    ring_s[d, s, n] = acc[d, n].astype(BF16)
                else:
                    ring_s[d, s] = (acc[d] + ring_r[d, s - 1].astype(F32)).astype(BF16)
                ring[d, s] = send(ring_s.at[d, s], ring_r.at[d, s], dev1(sign))
        product(0, p1)
        yield next(when)
        for d in range(2):
            ring[d, hops - 1].wait_recv()
        acc[0] = acc[0] + ring_r[0, hops - 1].astype(F32) + ring_r[1, hops - 1].astype(F32)
        dir_s[...] = acc[0].astype(BF16)
        direct = send_all(
            [(dir_s.at[(p2 + k) % n2], dir_r.at[k], dev2(k)) for k in range(1, n2)], dir_r.at[1:]
        )
        yield next(when)
        value = acc[0, p2]
        direct.wait_recv()
        for k in range(1, n2):
            value += dir_r[k].astype(F32)
        own_step(cs, value)
        mine = norm.at[z, h, :, cs]
        direct = send_all([(mine, mine, dev2(k)) for k in range(1, n2)], dir_r.at[1:])
        yield next(when)
        direct.wait_recv()
        back = {}
        for s in range(hops):
            for d in range(2):
                sign = 1 - 2 * d
                if s > 0:
                    back[d, s - 1].wait_recv()
                t = (p1 - sign * s + n1) % n1
                p = piece(t) if s < hops - 1 else piece(t, far[d])
                back[d, s] = send(p, p, dev1(sign))
            yield next(when)
        for d in range(2):
            back[d, hops - 1].wait_recv()
        expand(first, size)

    for c in loads[5:]:
        c.wait()
    lanes = [stream(f, w, axis, i * 0.3, bufs[5 * i : 5 * i + 5]) for i, (f, w, axis) in enumerate(STREAMS)]
    lanes.append(rows_stream())
    marks, settled = [], [0]

    def settle():
        marks.append(len(sends))
        if len(marks) > 2 * len(lanes):
            upto = marks[-2 * len(lanes) - 1]
            for c in sends[settled[0] : upto]:
                c.wait_send()
            settled[0] = upto

    queue = [(next(g), i, g) for i, g in enumerate(lanes)]
    while queue:
        queue.sort(key=lambda e: e[:2])
        _, i, g = queue.pop(0)
        t = next(g, None)
        if t is not None:
            queue.append((t, i, g))
        settle()

    @pl.when(is_0)
    def _():
        for i in range(n_down):
            down(i).wait_send()

    @pl.when(is_0 | is_1)
    def _():
        to_y.wait_send()

    @pl.when(same_core)
    def _():
        to_core.wait_send()

    for c in sends[settled[0] :]:
        c.wait_send()
    for c in stores:
        c.wait()


def copy_out(n, *refs):
    stage, sem = refs[2 * n : 3 * n], refs[-1]
    reads = [pltpu.make_async_copy(refs[i], stage[i], sem.at[i]) for i in range(n)]
    writes = [pltpu.make_async_copy(stage[i], refs[n + i], sem.at[n + i]) for i in range(n)]
    for c in reads:
        c.start()
    for r, w in zip(reads, writes):
        r.wait()
        w.start()
    for c in writes:
        c.wait()


def per_device(n_f, n_dp, tokens, logits, values, incoming, basis, gate_m, gate_s, lin_m, lin_s):
    n_h = Y_PARTS
    n_z = n_dp // n_h
    n_tok, depth = tokens.shape
    width = logits.shape[1]
    rank = basis.shape[1]
    own = rank // n_dp
    n_rows = basis.shape[0] * n_f // n_dp
    blk = rank // n_f
    dma = pltpu.SemaphoreType.DMA
    hbm = pl.BlockSpec(memory_space=pltpu.HBM)
    bufs = []
    n_sends = 4
    for _, size, axis in STREAMS:
        n1, n2 = (n_z, n_h) if axis == "z" else (n_h, n_z)
        n_sends += 2 * n1 + 2
        bufs += [
            pltpu.VMEM((2, n2, own, size), F32),
            pltpu.VMEM((2, n1 // 2, n2, own, size), BF16),
            pltpu.VMEM((2, n1 // 2, n2, own, size), BF16),
            pltpu.VMEM((n2, own, size), BF16),
            pltpu.VMEM((n2, own, size), BF16),
        ]
    outs = tuple(
        jax.ShapeDtypeStruct((r, width), F32) for r in (n_rows, n_rows, own, own, own, own)
    )
    done = pl.pallas_call(
        functools.partial(exchange, n_f, n_z, n_h),
        out_shape=outs,
        in_specs=[hbm] * 9,
        out_specs=(hbm,) * 6,
        scratch_shapes=[
            pltpu.VMEM((n_tok, depth), BF16),
            pltpu.VMEM(basis.shape, BF16),
            pltpu.VMEM((2, rank // 2, depth), BF16),
            pltpu.VMEM((n_tok, width), BF16),
            pltpu.VMEM((n_tok, width), BF16),
            pltpu.VMEM((n_tok, width), BF16),
            pltpu.VMEM((own, 2 * width), F32),
            pltpu.VMEM((own, 2 * width), F32),
            pltpu.VMEM((n_f // 2, blk, n_tok), F32),
            pltpu.VMEM((n_f // 2, blk, n_tok), F32),
            pltpu.VMEM((n_f // 2, blk, n_tok), F32),
            pltpu.VMEM((n_f // 2, blk, n_tok), BF16),
            pltpu.VMEM((n_f // 2, blk, n_tok), BF16),
            pltpu.VMEM((n_z, n_h, own, n_tok), BF16),
            pltpu.VMEM((n_tok, 2 * width), BF16),
            pltpu.VMEM((n_z, n_h, own, 2 * width), BF16),
            pltpu.VMEM((n_rows, rank), BF16),
            pltpu.VMEM((n_rows, 2 * width), F32),
            dma((9,)),
            dma((len(STREAMS) + 5,)),
            dma((n_sends,)),
            dma((n_sends,)),
            dma((n_f // 4 + 1,)),
            dma,
            *bufs,
        ],
        compiler_params=pltpu.CompilerParams(
            collective_id=0, has_side_effects=True, vmem_limit_bytes=64 * 1024 * 1024
        ),
    )(tokens, logits, values, incoming, basis, gate_m, gate_s, lin_m, lin_s)
    gate_u, lin_u, mg, sg, ml, sl = pl.pallas_call(
        functools.partial(copy_out, 6),
        out_shape=outs,
        in_specs=[hbm] * 6,
        out_specs=(hbm,) * 6,
        scratch_shapes=[pltpu.VMEM(o.shape, F32) for o in outs] + [dma((12,))],
    )(*done)
    return gate_u, lin_u, mg, sg, ml, sl


def solution(mesh):
    both = P("dp", "fsdp")
    return jax.shard_map(
        functools.partial(per_device, mesh.shape["fsdp"], mesh.shape["dp"]),
        mesh=mesh,
        in_specs=(both, both, both, both, P("fsdp", None), both, both, both, both),
        out_specs=(both,) * 6,
        check_vma=False,
    )
```
